128 devices in a mesh: dom: 8 (over z, x_lo), dp: 16 (over y, x_hi, core).
Axes of the slice: x: 4 (x_hi: 2, x_lo: 2; x = x_hi * 2 + x_lo), y: 4, z: 4, core: 2. Of those that a mesh axis runs over, the one named last changes fastest.
Arguments:
- state: bfloat16 [16, 8192, 512], P('dp', 'dom'), may hold values from -6 to 6
- blocks: bfloat16 [64, 4, 128, 128], P('dom'), may hold values from -0.25 to 0.25
- source: int32 [64, 4], P('dom'), may hold values from 0 to 11
- count: int32 [64], P('dom'), may hold values from 1 to 4, as said below
- cotangent: bfloat16 [16, 8192, 512], P('dp', 'dom'), may hold values from -6 to 6
- w_self: bfloat16 [3, 512, 512], replicated, may hold values from -0.25 to 0.25
- w_nbr: bfloat16 [3, 512, 512], replicated, may hold values from -0.25 to 0.25
Outputs:
- final_state: bfloat16 [16, 8192, 512], P('dp', 'dom')
- state_grad: bfloat16 [16, 8192, 512], P('dp', 'dom')
- self_grad: float32 [3, 512, 512], replicated
- nbr_grad: float32 [3, 512, 512], replicated
The draws below stay inside these ranges and needn't reach their ends.
Inputs may be any that keep to these rules, and one draw needn't show every extreme that they name: `source`: index into the partition's extended tiles: the last 2 tiles of the previous partition (cyclically), then its own 8 tiles, then the first 2 tiles of the next partition. Slots at or past the count are unused.
All inputs are finite; a program needn't handle non-finite values.
Results may differ from the reference program's by a relative error of at most 0.015.
Values may be sent and summed in bfloat16 or wider, within the bound.
No kernel may reach another device: no remote copies, remote signals or barrier semaphores. Data moves between devices by JAX's collectives and lax.ppermute only.
A program may use at most 128 MiB of HBM per device.

```python
import jax
import jax.numpy as jnp
from jax import lax

F = 512
TB = 128
TILE_DEV = 8
HALO = 2
NBR = 4
LAYERS = 3
TILES_TOTAL = 64
NODES = 8192
SAMPLES = 16


def draw_count(key, part):
    key = jax.random.fold_in(key, 7)
    tile_ids = jnp.arange(TILES_TOTAL, dtype=jnp.int32)
    topmost = 1 + tile_ids * NBR // TILES_TOTAL
    random_bits = jax.random.randint(key, (TILES_TOTAL,), 0, 1 << 20, dtype=jnp.int32)
    counts = 1 + random_bits % topmost
    return jnp.where(tile_ids == TILES_TOTAL - 1, NBR, counts).astype(jnp.int32)


def touch_ends(values, own_key, smallest, high):
    index_at = [jax.random.randint(jax.random.fold_in(own_key, axis), (), 0, length) for axis, length in enumerate(values.shape)]
    longest = values.shape.index(max(values.shape))
    next_to = index_at[:longest] + [(index_at[longest] + 1) % values.shape[longest]] + index_at[longest + 1:]
    return values.at[tuple(index_at)].set(smallest).at[tuple(next_to)].set(high)


def steps_of(own_key, dims, pieces, smallest, high):
    loudness = 1.0
    for position, blocks in pieces:
        draws = jax.random.uniform(jax.random.fold_in(jax.random.fold_in(own_key, 6), position), (blocks,), jnp.float32, smallest / len(pieces), high / len(pieces))
        loudness = loudness * jnp.repeat(jnp.exp(draws), dims[position] // blocks).reshape((-1,) + (1,) * (len(dims) - 1 - position))
    return loudness


def centred(rng, shape, scale, reach, pieces=(), kind=jnp.bfloat16):
    result = jax.random.normal(rng, shape, jnp.float32) * scale
    if len(pieces) > 0:
        result = steps_of(rng, shape, pieces, -0.22, 0.18) * result
    return jnp.clip(result, min=-reach, max=reach).astype(kind)


def setup_inputs(seed: int = 0) -> dict:
    seeds = jax.random.split(jax.random.key(seed), 8)
    state = centred(seeds[0], (SAMPLES, NODES, F), 1.0, 6.0, ((0, 16), (1, 8)))
    blocks = centred(seeds[1], (TILES_TOTAL, NBR, TB, TB), (TB * NBR) ** -0.5, 0.25, ((0, 8),))
    source = touch_ends(jax.random.randint(seeds[2], (TILES_TOTAL, NBR), 0, TILE_DEV + 2 * HALO), jax.random.fold_in(seeds[2], 1), 0, (TILE_DEV + 2 * HALO) - 1).astype(jnp.int32)
    count = draw_count(jax.random.fold_in(seeds[7], 71), 0)
    cotangent = centred(seeds[4], (SAMPLES, NODES, F), 1.0, 6.0, ((0, 16), (1, 8)))
    w_self = centred(seeds[5], (LAYERS, F, F), F ** -0.5, 0.25)
    w_nbr = centred(seeds[6], (LAYERS, F, F), F ** -0.5, 0.25)
    return dict(state=state, blocks=blocks, source=source, count=count, cotangent=cotangent, w_self=w_self, w_nbr=w_nbr)


def masked_blocks(blocks, count):
    live_slots = (jnp.arange(NBR, dtype=jnp.int32)[None, :] < count[:, None]).astype(jnp.bfloat16)
    return blocks * live_slots[:, :, None, None]


def reference(state, blocks, source, count, cotangent, w_self, w_nbr):
    weights_f = masked_blocks(blocks, count).astype(jnp.float32)
    owner = (jnp.arange(TILES_TOTAL, dtype=jnp.int32) // TILE_DEV) * TILE_DEV
    global_src = ((owner[:, None] + source - HALO) % TILES_TOTAL).astype(jnp.int32)
    flat_src = global_src.reshape(-1)

    def per_sample(totals, sample_pair):
        sample, cot_sample = sample_pair
        hidden = sample
        inputs, aggregates, preacts = [], [], []
        for stratum in range(LAYERS):
            tiles = hidden.reshape(TILES_TOTAL, TB, F).astype(jnp.float32)
            aggregate = jnp.einsum("tsab,tsbf->taf", weights_f, tiles[global_src]).reshape(NODES, F).astype(jnp.bfloat16)
            preact = jnp.dot(hidden, w_self[stratum], preferred_element_type=jnp.float32) + jnp.dot(aggregate, w_nbr[stratum], preferred_element_type=jnp.float32)
            inputs.append(hidden)
            aggregates.append(aggregate)
            preacts.append(preact)
            hidden = (hidden.astype(jnp.float32) + jax.nn.silu(preact)).astype(jnp.bfloat16)
        grad_now = cot_sample.astype(jnp.float32)
        self_parts, nbr_parts = [], []
        for stratum in reversed(range(LAYERS)):
            preact = preacts[stratum]
            sigmoid_pre = jax.nn.sigmoid(preact)
            grad_pre = (grad_now * sigmoid_pre * (1.0 + preact * (1.0 - sigmoid_pre))).astype(jnp.bfloat16)
            self_parts.append(jnp.dot(inputs[stratum].T, grad_pre, preferred_element_type=jnp.float32))
            nbr_parts.append(jnp.dot(aggregates[stratum].T, grad_pre, preferred_element_type=jnp.float32))
            grad_agg = jnp.dot(grad_pre, w_nbr[stratum].T, preferred_element_type=jnp.float32).astype(jnp.bfloat16)
            contrib = jnp.einsum("tsba,taf->tsbf", weights_f, grad_agg.reshape(TILES_TOTAL, TB, F).astype(jnp.float32))
            back = jax.ops.segment_sum(contrib.reshape(TILES_TOTAL * NBR, TB, F), flat_src, num_segments=TILES_TOTAL).reshape(NODES, F)
            grad_now = grad_now + jnp.dot(grad_pre, w_self[stratum].T, preferred_element_type=jnp.float32) + back
        self_stack = jnp.stack(self_parts[::-1])
        nbr_stack = jnp.stack(nbr_parts[::-1])
        return (totals[0] + self_stack, totals[1] + nbr_stack), (hidden, grad_now.astype(jnp.bfloat16))

    zeros_init = jnp.zeros((LAYERS, F, F), jnp.float32)
    sums, outputs = lax.scan(per_sample, (zeros_init, zeros_init), (state, cotangent))
    factor = float(SAMPLES * NODES) ** -0.5
    return outputs[0], outputs[1], sums[0] * factor, sums[1] * factor
```

```python
import functools
import math

import jax
import jax.numpy as jnp
from jax import lax
from jax.experimental import pallas as pl
from jax.experimental.pallas import tpu as pltpu
from jax.sharding import Mesh
from jax.sharding import PartitionSpec as P

LAYERS = 3
TB = 128
TILES = 8
SLOTS = 4
HALO = 2
F = 512
ROWS = TILES * TB
RIM = HALO * TB
EXT = TILES + 2 * HALO
BF = jnp.bfloat16
F32 = jnp.float32
EDGE = (0, 1, 6, 7)
MID = (2, 3, 4, 5)
MB = 1 << 20

SM = pl.BlockSpec(memory_space=pltpu.SMEM)
VM = pl.BlockSpec(memory_space=pltpu.VMEM)


def pinned(shape, dtype):
    return pltpu.VMEM(shape, dtype)


def call(body, name, out_shape, in_specs, scratch=(), macs=0):
    return pl.pallas_call(
        body,
        name=name,
        out_shape=out_shape,
        in_specs=in_specs,
        out_specs=jax.tree.map(lambda _: VM, out_shape, is_leaf=lambda x: hasattr(x, "shape")),
        scratch_shapes=list(scratch),
        compiler_params=pltpu.CompilerParams(vmem_limit_bytes=12 * MB),
        cost_estimate=pl.CostEstimate(flops=2 * macs, bytes_accessed=4 * MB, transcendentals=0),
    )


def rows(tile):
    return slice(tile * TB, (tile + 1) * TB)


def dot(a, b):
    return jnp.dot(a, b, preferred_element_type=F32)


def dot_nt(a, b):
    return lax.dot_general(a, b, (((1,), (1,)), ((), ())), preferred_element_type=F32)


def dot_tn(a, b):
    return lax.dot_general(a, b, (((0,), (0,)), ((), ())), preferred_element_type=F32)


def fill_ext(ext, lo, hidden, hi):
    ext[0:RIM, :] = lo[...]
    ext[RIM : RIM + ROWS, :] = hidden[...]
    ext[RIM + ROWS :, :] = hi[...]


def gather(source, ext, tile):
    return jnp.concatenate(
        [ext[pl.ds(pl.multiple_of(source[tile, s] * TB, TB), TB), :] for s in range(SLOTS)], axis=0
    )


def act(pre):
    sig = 0.5 * jnp.tanh(0.5 * pre) + 0.5
    return pre * sig, sig * (1.0 + pre * (1.0 - sig))


def scatter(source, adj_v, grad_agg, back, tile):
    part = dot(adj_v[tile], grad_agg)
    for s in range(SLOTS):
        at = pl.ds(pl.multiple_of(source[tile, s] * TB, TB), TB)
        back[at, :] += part[s * TB : (s + 1) * TB, :]


def prepare(count, blocks, state, w_self, w_nbr, adj, adj_v, own, *kept):
    for layer in range(LAYERS):
        kept[layer][...] = w_self[layer]
        kept[LAYERS + layer][...] = w_nbr[layer]
    for t in range(TILES):
        for s in range(SLOTS):
            live = (s < count[t]).astype(F32)
            block = blocks[t, s].astype(F32) * live
            adj[t, :, s * TB : (s + 1) * TB] = block.astype(BF)
            adj_v[t, s * TB : (s + 1) * TB, :] = block.astype(BF)
    own[...] = dot(state[...], w_self[0])


def forward_pair(source, adj, ext, own, hidden, w_nbr, pair):
    agg = jnp.concatenate([dot(adj[t], gather(source, ext, t)) for t in pair], axis=0).astype(BF)
    at = slice(pair[0] * TB, (pair[-1] + 1) * TB)
    pre = own[at, :] + dot(agg, w_nbr[...])
    gain, slope = act(pre)
    new = (hidden[at, :].astype(F32) + gain).astype(BF)
    return agg, new, slope


def forward_edge(source, adj, lo, hi, hidden, own, w_nbr, new_lo, new_hi, agg_e, slope_e, ext):
    fill_ext(ext, lo, hidden, hi)
    for i, (pair, out) in enumerate((((0, 1), new_lo), ((6, 7), new_hi))):
        agg, new, slope = forward_pair(source, adj, ext, own, hidden, w_nbr, pair)
        out[...] = new
        agg_e[i * RIM : (i + 1) * RIM, :] = agg
        slope_e[i * RIM : (i + 1) * RIM, :] = slope


def forward_mid(
    source, adj, lo, hi, hidden, own, w_nbr, new_lo, new_hi, agg_e, slope_e, w_self,
    new, agg_o, slope_o, own_o, ext,
):
    fill_ext(ext, lo, hidden, hi)
    for pair in ((2, 3), (4, 5)):
        at = slice(pair[0] * TB, (pair[-1] + 1) * TB)
        agg_o[at, :], new[at, :], slope_o[at, :] = forward_pair(
            source, adj, ext, own, hidden, w_nbr, pair
        )
    for i, edge in enumerate((new_lo, new_hi)):
        at = slice(i * (ROWS - RIM), i * (ROWS - RIM) + RIM)
        new[at, :] = edge[...]
        agg_o[at, :] = agg_e[i * RIM : (i + 1) * RIM, :]
        slope_o[at, :] = slope_e[i * RIM : (i + 1) * RIM, :]
    own_o[...] = dot(new[...], w_self[...])


def turn(
    source, adj, adj_v, lo, hi, hidden, own, w_nbr, cot,
    final, agg_o, gp_o, back, rim_lo, rim_hi, ext,
):
    fill_ext(ext, lo, hidden, hi)
    back[...] = jnp.zeros_like(back)
    for first in range(0, TILES, 2):
        pair = (first, first + 1)
        at = slice(pair[0] * TB, (pair[-1] + 1) * TB)
        agg, new, slope = forward_pair(source, adj, ext, own, hidden, w_nbr, pair)
        agg_o[at, :] = agg
        final[at, :] = new
        gp = (cot[at, :].astype(F32) * slope).astype(BF)
        gp_o[at, :] = gp
        grad_agg = dot_nt(gp, w_nbr[...]).astype(BF)
        for i, t in enumerate(pair):
            scatter(source, adj_v, grad_agg[i * TB : (i + 1) * TB], back, t)
    rim_lo[...] = back[0:RIM, :].astype(BF)
    rim_hi[...] = back[RIM + ROWS :, :].astype(BF)


def backward_mid(source, adj_v, gp, grad, back, w_self, slope, w_nbr, grad_o, gp_m, part):
    grad_o[...] = (
        grad[...].astype(F32) + dot_nt(gp[...], w_self[...]) + back[RIM : RIM + ROWS, :]
    )
    part[...] = jnp.zeros_like(part)
    for pair in ((2, 3), (4, 5)):
        at = slice(pair[0] * TB, (pair[-1] + 1) * TB)
        new = (grad_o[at, :] * slope[at, :]).astype(BF)
        gp_m[at.start - RIM : at.stop - RIM, :] = new
        grad_agg = dot_nt(new, w_nbr[...]).astype(BF)
        for i, t in enumerate(pair):
            scatter(source, adj_v, grad_agg[i * TB : (i + 1) * TB], part, t)


def backward_edge(
    source, adj_v, from_prev, from_next, grad, slope, w_nbr, gp_m, part,
    grad_o, gp_o, back, rim_lo, rim_hi,
):
    back[...] = part[...]
    for pair, come in (((0, 1), from_prev), ((6, 7), from_next)):
        at = slice(pair[0] * TB, (pair[-1] + 1) * TB)
        total = grad[at, :] + come[...].astype(F32)
        grad_o[at, :] = total
        new = (total * slope[at, :]).astype(BF)
        gp_o[at, :] = new
        grad_agg = dot_nt(new, w_nbr[...]).astype(BF)
        for i, t in enumerate(pair):
            scatter(source, adj_v, grad_agg[i * TB : (i + 1) * TB], back, t)
    rim_lo[...] = back[0:RIM, :].astype(BF)
    rim_hi[...] = back[RIM + ROWS :, :].astype(BF)
    grad_o[RIM : ROWS - RIM, :] = grad[RIM : ROWS - RIM, :]
    gp_o[RIM : ROWS - RIM, :] = gp_m[...]


def backward_first(gp, grad, back, w_self, grad_o):
    grad_o[...] = grad[...] + dot_nt(gp[...], w_self[...]) + back[RIM : RIM + ROWS, :]


def backward_last(grad, from_prev, from_next, out):
    out[0:RIM, :] = (grad[0:RIM, :] + from_prev[...].astype(F32)).astype(BF)
    out[RIM : ROWS - RIM, :] = grad[RIM : ROWS - RIM, :].astype(BF)
    out[ROWS - RIM :, :] = (grad[ROWS - RIM :, :] + from_next[...].astype(F32)).astype(BF)


def weight_grad(core, hidden, agg, gp, keep, send):
    for i, left in enumerate((hidden, agg)):
        full = dot_tn(left[...], gp[...]).astype(BF)
        low, high = full[:, : F // 2], full[:, F // 2 :]
        first = jnp.broadcast_to(core[0] == 0, low.shape)
        keep[i * F : (i + 1) * F, :] = jnp.where(first, low, high)
        send[i * F : (i + 1) * F, :] = jnp.where(first, high, low)


def add_halves(mine, other, out):
    out[...] = (mine[...].astype(F32) + other[...].astype(F32)).astype(BF)


def sum_parts(parts, out):
    total = parts[0].astype(F32)
    for i in range(1, parts.shape[0]):
        total += parts[i].astype(F32)
    out[...] = total.astype(BF)


def unpack(factor, core, mine, other, self_o, nbr_o):
    for i, out in enumerate((self_o, nbr_o)):
        a = mine[i * F : (i + 1) * F, :].astype(F32) * factor
        b = other[i * F : (i + 1) * F, :].astype(F32) * factor
        first = jnp.broadcast_to(core[0] == 0, a.shape)
        out[:, : F // 2] = jnp.where(first, a, b)
        out[:, F // 2 :] = jnp.where(first, b, a)


def per_device(state, blocks, source, count, cotangent, w_self, w_nbr):
    state = state.reshape(ROWS, F)
    cotangent = cotangent.reshape(ROWS, F)
    n_dom = lax.axis_size("dom")
    up = [(i, (i + 1) % n_dom) for i in range(n_dom)]
    down = [(i, (i - 1) % n_dom) for i in range(n_dom)]
    core = lax.axis_index("core").astype(jnp.int32).reshape(1)
    peers = lax.axis_size("dom") * lax.axis_size("dq")

    def swap(to_prev, to_next):
        return lax.ppermute(to_next, "dom", up), lax.ppermute(to_prev, "dom", down)

    wide = jax.ShapeDtypeStruct((RIM, F), BF)
    ext_scratch = pltpu.VMEM((EXT * TB, F), BF)
    unit = ROWS * F * F

    lo, hi = swap(state[:RIM], state[ROWS - RIM :])
    adj, adj_v, own, *kept = call(
        prepare, "prepare",
        (
            pinned((TILES, TB, SLOTS * TB), BF), pinned((TILES, SLOTS * TB, TB), BF),
            pinned((ROWS, F), F32), *[pinned((F, F), BF)] * (2 * LAYERS),
        ),
        [SM] + [VM] * 4, macs=unit,
    )(count, blocks, state, w_self, w_nbr)
    w_self, w_nbr = kept[:LAYERS], kept[LAYERS:]

    hidden = state
    hiddens, aggs, slopes = [], [], []
    for layer in range(LAYERS - 1):
        new_lo, new_hi, agg_e, slope_e = call(
            forward_edge, f"forward_edge{layer}",
            (wide, wide, pinned((2 * RIM, F), BF), pinned((2 * RIM, F), F32)),
            [SM] + [VM] * 6, [ext_scratch], macs=unit,
        )(source, adj, lo, hi, hidden, own, w_nbr[layer])
        next_lo, next_hi = swap(new_lo, new_hi)
        new, agg, slope, own = call(
            forward_mid, f"forward_mid{layer}",
            (pinned((ROWS, F), BF), pinned((ROWS, F), BF), pinned((ROWS, F), F32), pinned((ROWS, F), F32)),
            [SM] + [VM] * 11, [ext_scratch], macs=2 * unit,
        )(
            source, adj, lo, hi, hidden, own, w_nbr[layer], new_lo, new_hi, agg_e, slope_e,
            w_self[layer + 1],
        )
        hiddens.append(hidden)
        aggs.append(agg)
        slopes.append(slope)
        hidden, lo, hi = new, next_lo, next_hi

    hiddens.append(hidden)
    top = LAYERS - 1
    final, agg, gp, back, rim_lo, rim_hi = call(
        turn, "turn",
        (
            jax.ShapeDtypeStruct((ROWS, F), BF), pinned((ROWS, F), BF), pinned((ROWS, F), BF),
            pinned((EXT * TB, F), F32), wide, wide,
        ),
        [SM] + [VM] * 8, [ext_scratch], macs=4 * unit,
    )(source, adj, adj_v, lo, hi, hidden, own, w_nbr[top], cotangent)
    aggs.append(agg)
    grad = cotangent

    def weights(layer, gp):
        half = (ROWS, F // 2)
        out = jax.ShapeDtypeStruct(half, BF)
        keep, send = call(
            weight_grad, f"weight_grad{layer}", (out, out), [SM, VM, VM, VM], macs=2 * unit
        )(core, hiddens[layer], aggs[layer], gp)
        got = lax.ppermute(send, "core", [(0, 1), (1, 0)])
        return call(add_halves, f"add_halves{layer}", out, [VM, VM])(keep, got)

    def reduce(layer, chip):
        half = (ROWS, F // 2)
        depth = ROWS // peers
        parts = lax.all_to_all(
            chip.reshape(peers, depth, F // 2), ("dom", "dq"), 0, 0, tiled=True
        )
        mine = call(
            sum_parts, f"sum_parts{layer}", jax.ShapeDtypeStruct((depth, F // 2), BF), [VM]
        )(parts)
        whole = lax.all_to_all(
            jnp.broadcast_to(mine[None], parts.shape), ("dom", "dq"), 0, 0, tiled=True
        ).reshape(half)
        other = lax.ppermute(whole, "core", [(0, 1), (1, 0)])
        total_rows = lax.axis_size("dq") * lax.axis_size("core") * n_dom * ROWS
        grads = jax.ShapeDtypeStruct((F, F), F32)
        return call(
            functools.partial(unpack, 1.0 / math.sqrt(total_rows)), f"unpack{layer}",
            (grads, grads), [SM, VM, VM],
        )(core, whole, other)

    results = []
    for layer in range(top, 0, -1):
        from_prev, from_next = swap(rim_lo, rim_hi)
        chip = weights(layer, gp)
        grad, gp_m, part = call(
            backward_mid, f"backward_mid{layer}",
            (pinned((ROWS, F), F32), pinned((ROWS - 2 * RIM, F), BF), pinned((EXT * TB, F), F32)),
            [SM] + [VM] * 7, macs=3 * unit,
        )(source, adj_v, gp, grad, back, w_self[layer], slopes[layer - 1], w_nbr[layer - 1])
        grad, gp, back, rim_lo, rim_hi = call(
            backward_edge, f"backward_edge{layer - 1}",
            (pinned((ROWS, F), F32), pinned((ROWS, F), BF), pinned((EXT * TB, F), F32), wide, wide),
            [SM] + [VM] * 8, macs=unit,
        )(source, adj_v, from_prev, from_next, grad, slopes[layer - 1], w_nbr[layer - 1], gp_m, part)
        results.append(reduce(layer, chip))

    from_prev, from_next = swap(rim_lo, rim_hi)
    chip = weights(0, gp)
    grad = call(
        backward_first, "backward_first", pinned((ROWS, F), F32), [VM] * 4, macs=unit
    )(gp, grad, back, w_self[0])
    results.append(reduce(0, chip))
    state_grad = call(
        backward_last, "backward_last", jax.ShapeDtypeStruct((ROWS, F), BF), [VM] * 3
    )(grad, from_prev, from_next)
    results = results[::-1]
    return (
        final[None],
        state_grad[None],
        jnp.stack([r[0] for r in results]),
        jnp.stack([r[1] for r in results]),
    )


def solution(mesh):
    dom, dp = mesh.devices.shape
    fine = Mesh(mesh.devices.reshape(dom, dp // 2, 2), ("dom", "dq", "core"))
    nodes = P(("dq", "core"), "dom", None)
    in_specs = (nodes, P("dom", None, None, None), P("dom", None), P("dom"), nodes, P(), P())
    out_specs = (nodes, nodes, P(), P())
    return jax.shard_map(
        per_device, mesh=fine, in_specs=in_specs, out_specs=out_specs, check_vma=False
    )
```

```python
import functools
import math

import jax
import jax.numpy as jnp
from jax import lax
from jax.experimental import pallas as pl
from jax.experimental.pallas import tpu as pltpu
from jax.sharding import Mesh
from jax.sharding import PartitionSpec as P

LAYERS = 3
TB = 128
TILES = 8
SLOTS = 4
HALO = 2
F = 512
ROWS = TILES * TB
RIM = HALO * TB
EXT = TILES + 2 * HALO
BF = jnp.bfloat16
F32 = jnp.float32
EDGE = (0, 1, 6, 7)
MID = (2, 3, 4, 5)
MB = 1 << 20

SM = pl.BlockSpec(memory_space=pltpu.SMEM)
VM = pl.BlockSpec(memory_space=pltpu.VMEM)
HB = pl.BlockSpec(memory_space=pltpu.HBM)


def pinned(shape, dtype):
    return pltpu.VMEM(shape, dtype)


def call(body, name, out_shape, in_specs, scratch=()):
    return pl.pallas_call(
        body,
        name=name,
        out_shape=out_shape,
        in_specs=in_specs,
        out_specs=jax.tree.map(lambda _: VM, out_shape, is_leaf=lambda x: hasattr(x, "shape")),
        scratch_shapes=list(scratch),
        compiler_params=pltpu.CompilerParams(vmem_limit_bytes=12 * MB),
        cost_estimate=pl.CostEstimate(flops=1, bytes_accessed=1, transcendentals=0),
    )


def rows(tile):
    return slice(tile * TB, (tile + 1) * TB)


def dot(a, b):
    return jnp.dot(a, b, preferred_element_type=F32)


def dot_nt(a, b):
    return lax.dot_general(a, b, (((1,), (1,)), ((), ())), preferred_element_type=F32)


def dot_tn(a, b):
    return lax.dot_general(a, b, (((0,), (0,)), ((), ())), preferred_element_type=F32)


def fill_ext(ext, lo, hidden, hi):
    ext[0:RIM, :] = lo[...]
    ext[RIM : RIM + ROWS, :] = hidden[...]
    ext[RIM + ROWS :, :] = hi[...]


def gather(source, ext, tile):
    return jnp.concatenate(
        [ext[pl.ds(pl.multiple_of(source[s, tile] * TB, TB), TB), :] for s in range(SLOTS)], axis=0
    )


def act(pre):
    sig = 0.5 * jnp.tanh(0.5 * pre) + 0.5
    return pre * sig, sig * (1.0 + pre * (1.0 - sig))


def scatter(source, adj_v, grad_agg, back, tile):
    part = dot(adj_v[tile], grad_agg)
    for s in range(SLOTS):
        at = pl.ds(pl.multiple_of(source[s, tile] * TB, TB), TB)
        back[at, :] += part[s * TB : (s + 1) * TB, :]


def edge_tiles(state, lo, hi, sems):
    copies = [
        pltpu.make_async_copy(state.at[pl.ds(0, RIM), :], lo, sems.at[0]),
        pltpu.make_async_copy(state.at[pl.ds(ROWS - RIM, RIM), :], hi, sems.at[1]),
    ]
    for copy in copies:
        copy.start()
    for copy in copies:
        copy.wait()


def prepare(count, blocks, state, w_self, w_nbr, adj, adj_v, own, hidden, *rest):
    kept, (raw, sems) = rest[: 2 * LAYERS], rest[2 * LAYERS :]
    loads = [(state, hidden), (w_self.at[0], kept[0]), (blocks, raw)]
    for layer in range(LAYERS):
        if layer:
            loads.append((w_self.at[layer], kept[layer]))
        loads.append((w_nbr.at[layer], kept[LAYERS + layer]))
    copies = [pltpu.make_async_copy(a, b, sems.at[i]) for i, (a, b) in enumerate(loads)]
    for copy in copies:
        copy.start()
    copies[0].wait()
    copies[1].wait()
    own[...] = dot(hidden[...], kept[0][...])
    copies[2].wait()
    for t in range(TILES):
        for s in range(SLOTS):
            live = (s < count[t]).astype(F32)
            block = (raw[t, s].astype(F32) * live).astype(BF)
            adj[t, :, s * TB : (s + 1) * TB] = block
            adj_v[t, s * TB : (s + 1) * TB, :] = block
    for copy in copies[3:]:
        copy.wait()


def forward_pair(source, adj, ext, own, hidden, w_nbr, pair):
    agg = jnp.concatenate([dot(adj[t], gather(source, ext, t)) for t in pair], axis=0).astype(BF)
    at = slice(pair[0] * TB, (pair[-1] + 1) * TB)
    pre = own[at, :] + dot(agg, w_nbr[...])
    gain, slope = act(pre)
    new = (hidden[at, :].astype(F32) + gain).astype(BF)
    return agg, new, slope


def forward_edge(source, adj, lo, hi, hidden, own, w_nbr, new_lo, new_hi, agg_e, slope_e, ext):
    fill_ext(ext, lo, hidden, hi)
    for i, (pair, out) in enumerate((((0, 1), new_lo), ((6, 7), new_hi))):
        agg, new, slope = forward_pair(source, adj, ext, own, hidden, w_nbr, pair)
        out[...] = new
        agg_e[i * RIM : (i + 1) * RIM, :] = agg
        slope_e[i * RIM : (i + 1) * RIM, :] = slope


def forward_mid(
    source, adj, lo, hi, hidden, own, w_nbr, new_lo, new_hi, agg_e, slope_e, w_self,
    new, agg_o, slope_o, own_o, ext,
):
    fill_ext(ext, lo, hidden, hi)
    for pair in ((2, 3), (4, 5)):
        at = slice(pair[0] * TB, (pair[-1] + 1) * TB)
        agg_o[at, :], new[at, :], slope_o[at, :] = forward_pair(
            source, adj, ext, own, hidden, w_nbr, pair
        )
    for i, edge in enumerate((new_lo, new_hi)):
        at = slice(i * (ROWS - RIM), i * (ROWS - RIM) + RIM)
        new[at, :] = edge[...]
        agg_o[at, :] = agg_e[i * RIM : (i + 1) * RIM, :]
        slope_o[at, :] = slope_e[i * RIM : (i + 1) * RIM, :]
    own_o[...] = dot(new[...], w_self[...])


def turn(
    source, adj, adj_v, lo, hi, hidden, own, w_nbr, cot,
    final, agg_o, gp_o, back, rim_lo, rim_hi, ext,
):
    fill_ext(ext, lo, hidden, hi)
    back[...] = jnp.zeros_like(back)
    for first in range(0, TILES, 2):
        pair = (first, first + 1)
        at = slice(pair[0] * TB, (pair[-1] + 1) * TB)
        agg, new, slope = forward_pair(source, adj, ext, own, hidden, w_nbr, pair)
        agg_o[at, :] = agg
        final[at, :] = new
        gp = (cot[at, :].astype(F32) * slope).astype(BF)
        gp_o[at, :] = gp
        grad_agg = dot_nt(gp, w_nbr[...]).astype(BF)
        for i, t in enumerate(pair):
            scatter(source, adj_v, grad_agg[i * TB : (i + 1) * TB], back, t)
    rim_lo[...] = back[0:RIM, :].astype(BF)
    rim_hi[...] = back[RIM + ROWS :, :].astype(BF)


def backward_mid(source, adj_v, gp, grad, back, w_self, slope, w_nbr, grad_o, gp_m, part):
    grad_o[...] = (
        grad[...].astype(F32) + dot_nt(gp[...], w_self[...]) + back[RIM : RIM + ROWS, :]
    )
    part[...] = jnp.zeros_like(part)
    for pair in ((2, 3), (4, 5)):
        at = slice(pair[0] * TB, (pair[-1] + 1) * TB)
        new = (grad_o[at, :] * slope[at, :]).astype(BF)
        gp_m[at.start - RIM : at.stop - RIM, :] = new
        grad_agg = dot_nt(new, w_nbr[...]).astype(BF)
        for i, t in enumerate(pair):
            scatter(source, adj_v, grad_agg[i * TB : (i + 1) * TB], part, t)


def backward_edge(
    source, adj_v, from_prev, from_next, grad, slope, w_nbr, gp_m, part,
    grad_o, gp_o, back, rim_lo, rim_hi,
):
    back[...] = part[...]
    for pair, come in (((0, 1), from_prev), ((6, 7), from_next)):
        at = slice(pair[0] * TB, (pair[-1] + 1) * TB)
        total = grad[at, :] + come[...].astype(F32)
        grad_o[at, :] = total
        new = (total * slope[at, :]).astype(BF)
        gp_o[at, :] = new
        grad_agg = dot_nt(new, w_nbr[...]).astype(BF)
        for i, t in enumerate(pair):
            scatter(source, adj_v, grad_agg[i * TB : (i + 1) * TB], back, t)
    rim_lo[...] = back[0:RIM, :].astype(BF)
    rim_hi[...] = back[RIM + ROWS :, :].astype(BF)
    grad_o[RIM : ROWS - RIM, :] = grad[RIM : ROWS - RIM, :]
    gp_o[RIM : ROWS - RIM, :] = gp_m[...]


def backward_first(gp, grad, back, w_self, grad_o):
    grad_o[...] = grad[...] + dot_nt(gp[...], w_self[...]) + back[RIM : RIM + ROWS, :]


def backward_last(grad, from_prev, from_next, out):
    out[0:RIM, :] = (grad[0:RIM, :] + from_prev[...].astype(F32)).astype(BF)
    out[RIM : ROWS - RIM, :] = grad[RIM : ROWS - RIM, :].astype(BF)
    out[ROWS - RIM :, :] = (grad[ROWS - RIM :, :] + from_next[...].astype(F32)).astype(BF)


def weight_grad(hidden, agg, gp, keep, send):
    core = lax.axis_index("core")
    for i, left in enumerate((hidden, agg)):
        full = dot_tn(left[...], gp[...]).astype(BF)
        low, high = full[:, : F // 2], full[:, F // 2 :]
        first = jnp.broadcast_to(core == 0, low.shape)
        keep[i * F : (i + 1) * F, :] = jnp.where(first, low, high)
        send[i * F : (i + 1) * F, :] = jnp.where(first, high, low)


def add_halves(mine, other, out):
    out[...] = (mine[...].astype(F32) + other[...].astype(F32)).astype(BF)


def all_parts(*refs):
    out = refs[-1]
    depth = out.shape[1] // LAYERS
    for layer in range(LAYERS):
        if layer:
            chip = refs[layer + 1][...]
        else:
            chip = (refs[0][...].astype(F32) + refs[1][...].astype(F32)).astype(BF)
        for i in range(out.shape[0]):
            out[i, layer * depth : (layer + 1) * depth, :] = chip[i * depth : (i + 1) * depth, :]


def sum_parts(parts, out):
    total = parts[0].astype(F32)
    for i in range(1, parts.shape[0]):
        total += parts[i].astype(F32)
    total = total.astype(BF)
    for i in range(out.shape[0]):
        out[i] = total


def unpack(factor, mine, other, *outs):
    core = lax.axis_index("core")
    depth = mine.shape[1] // LAYERS
    for layer in range(LAYERS):
        at = slice(layer * depth, (layer + 1) * depth)
        for i, out in enumerate(outs):
            group = slice(i * F // depth, (i + 1) * F // depth)
            a = mine[group, at, :].reshape(F, F // 2).astype(F32) * factor
            b = other[group, at, :].reshape(F, F // 2).astype(F32) * factor
            first = jnp.broadcast_to(core == 0, a.shape)
            out[layer, :, : F // 2] = jnp.where(first, a, b)
            out[layer, :, F // 2 :] = jnp.where(first, b, a)


def per_device(state, blocks, source, count, cotangent, w_self, w_nbr):
    state = state.reshape(ROWS, F)
    source = source.T
    cotangent = cotangent.reshape(ROWS, F)
    n_dom = lax.axis_size("dom")
    up = [(i, (i + 1) % n_dom) for i in range(n_dom)]
    down = [(i, (i - 1) % n_dom) for i in range(n_dom)]
    peers = lax.axis_size("dom") * lax.axis_size("dq")

    def swap(to_prev, to_next):
        return lax.ppermute(to_next, "dom", up), lax.ppermute(to_prev, "dom", down)

    wide = jax.ShapeDtypeStruct((RIM, F), BF)
    ext_scratch = pltpu.VMEM((EXT * TB, F), BF)

    lo, hi = swap(
        *call(edge_tiles, "edge_tiles", (wide, wide), [HB], [pltpu.SemaphoreType.DMA((2,))])(state)
    )
    adj, adj_v, own, hidden, *kept = call(
        prepare, "prepare",
        (
            pinned((TILES, TB, SLOTS * TB), BF), pinned((TILES, SLOTS * TB, TB), BF),
            pinned((ROWS, F), F32), pinned((ROWS, F), BF), *[pinned((F, F), BF)] * (2 * LAYERS),
        ),
        [SM] + [HB] * 4,
        [pltpu.VMEM((TILES, SLOTS, TB, TB), BF), pltpu.SemaphoreType.DMA((2 * LAYERS + 2,))],
    )(count, blocks, state, w_self, w_nbr)
    w_self, w_nbr = kept[:LAYERS], kept[LAYERS:]

    hiddens, aggs, slopes = [], [], []
    for layer in range(LAYERS - 1):
        new_lo, new_hi, agg_e, slope_e = call(
            forward_edge, f"forward_edge{layer}",
            (wide, wide, pinned((2 * RIM, F), BF), pinned((2 * RIM, F), F32)),
            [SM] + [VM] * 6, [ext_scratch],
        )(source, adj, lo, hi, hidden, own, w_nbr[layer])
        next_lo, next_hi = swap(new_lo, new_hi)
        new, agg, slope, own = call(
            forward_mid, f"forward_mid{layer}",
            (pinned((ROWS, F), BF), pinned((ROWS, F), BF), pinned((ROWS, F), F32), pinned((ROWS, F), F32)),
            [SM] + [VM] * 11, [ext_scratch],
        )(
            source, adj, lo, hi, hidden, own, w_nbr[layer], new_lo, new_hi, agg_e, slope_e,
            w_self[layer + 1],
        )
        hiddens.append(hidden)
        aggs.append(agg)
        slopes.append(slope)
        hidden, lo, hi = new, next_lo, next_hi

    hiddens.append(hidden)
    top = LAYERS - 1
    final, agg, gp, back, rim_lo, rim_hi = call(
        turn, "turn",
        (
            jax.ShapeDtypeStruct((ROWS, F), BF), pinned((ROWS, F), BF), pinned((ROWS, F), BF),
            pinned((EXT * TB, F), F32), wide, wide,
        ),
        [SM] + [VM] * 8, [ext_scratch],
    )(source, adj, adj_v, lo, hi, hidden, own, w_nbr[top], cotangent)
    aggs.append(agg)
    grad = cotangent

    half = jax.ShapeDtypeStruct((ROWS, F // 2), BF)
    pieces = jax.ShapeDtypeStruct((peers, LAYERS * ROWS // peers, F // 2), BF)
    flip = [(0, 1), (1, 0)]

    def weights(layer, gp):
        keep, send = call(weight_grad, f"weight_grad{layer}", (half, half), [VM] * 3)(
            hiddens[layer], aggs[layer], gp
        )
        return keep, lax.ppermute(send, "core", flip)

    def spread(array):
        return lax.all_to_all(array, ("dom", "dq"), 0, 0, tiled=True)

    chips = []
    for layer in range(top, -1, -1):
        from_prev, from_next = swap(rim_lo, rim_hi)
        keep, got = weights(layer, gp)
        if layer:
            chips.append(call(add_halves, f"add_halves{layer}", half, [VM] * 2)(keep, got))
            grad, gp_m, part = call(
                backward_mid, f"backward_mid{layer}",
                (pinned((ROWS, F), F32), pinned((ROWS - 2 * RIM, F), BF), pinned((EXT * TB, F), F32)),
                [SM] + [VM] * 7,
            )(source, adj_v, gp, grad, back, w_self[layer], slopes[layer - 1], w_nbr[layer - 1])
            grad, gp, back, rim_lo, rim_hi = call(
                backward_edge, f"backward_edge{layer - 1}",
                (pinned((ROWS, F), F32), pinned((ROWS, F), BF), pinned((EXT * TB, F), F32), wide, wide),
                [SM] + [VM] * 8,
            )(source, adj_v, from_prev, from_next, grad, slopes[layer - 1], w_nbr[layer - 1], gp_m, part)
    grad = call(
        backward_first, "backward_first", jax.ShapeDtypeStruct((ROWS, F), F32), [VM] * 4
    )(gp, grad, back, w_self[0])
    parts = spread(call(all_parts, "all_parts", pieces, [VM] * 4)(keep, got, *chips[::-1]))
    state_grad = call(
        backward_last, "backward_last", jax.ShapeDtypeStruct((ROWS, F), BF), [VM] * 3
    )(grad, from_prev, from_next)
    out = call(sum_parts, "sum_parts", pieces, [VM])(parts)
    out, state_grad = lax.optimization_barrier((out, state_grad))
    whole = spread(out)
    other = lax.ppermute(whole, "core", flip)
    total_rows = lax.axis_size("dq") * lax.axis_size("core") * n_dom * ROWS
    grads = jax.ShapeDtypeStruct((LAYERS, F, F), F32)
    self_grad, nbr_grad = call(
        functools.partial(unpack, 1.0 / math.sqrt(total_rows)), "unpack", (grads, grads), [VM] * 2
    )(whole, other)
    return final[None], state_grad[None], self_grad, nbr_grad


def solution(mesh):
    dom, dp = mesh.devices.shape
    fine = Mesh(mesh.devices.reshape(dom, dp // 2, 2), ("dom", "dq", "core"))
    nodes = P(("dq", "core"), "dom", None)
    in_specs = (nodes, P("dom", None, None, None), P("dom", None), P("dom"), nodes, P(), P())
    out_specs = (nodes, nodes, P(), P())
    return jax.shard_map(
        per_device, mesh=fine, in_specs=in_specs, out_specs=out_specs, check_vma=False
    )
```

```python
import functools
import math

import jax
import jax.numpy as jnp
from jax import lax
from jax.experimental import pallas as pl
from jax.experimental.pallas import tpu as pltpu
from jax.sharding import Mesh
from jax.sharding import PartitionSpec as P

LAYERS = 3
TB = 128
TILES = 8
SLOTS = 4
HALO = 2
F = 512
ROWS = TILES * TB
RIM = HALO * TB
EXT = TILES + 2 * HALO
BF = jnp.bfloat16
F32 = jnp.float32
EDGE = (0, 1, 6, 7)
MID = (2, 3, 4, 5)
MB = 1 << 20

SM = pl.BlockSpec(memory_space=pltpu.SMEM)
VM = pl.BlockSpec(memory_space=pltpu.VMEM)
HB = pl.BlockSpec(memory_space=pltpu.HBM)


def pinned(shape, dtype):
    return pltpu.VMEM(shape, dtype)


def call(body, name, out_shape, in_specs, scratch=()):
    return pl.pallas_call(
        body,
        name=name,
        out_shape=out_shape,
        in_specs=in_specs,
        out_specs=jax.tree.map(lambda _: VM, out_shape, is_leaf=lambda x: hasattr(x, "shape")),
        scratch_shapes=list(scratch),
        compiler_params=pltpu.CompilerParams(vmem_limit_bytes=12 * MB),
        cost_estimate=pl.CostEstimate(flops=1, bytes_accessed=1, transcendentals=0),
    )


def rows(tile):
    return slice(tile * TB, (tile + 1) * TB)


def dot(a, b):
    return jnp.dot(a, b, preferred_element_type=F32)


def dot_nt(a, b):
    return lax.dot_general(a, b, (((1,), (1,)), ((), ())), preferred_element_type=F32)


def dot_tn(a, b):
    return lax.dot_general(a, b, (((0,), (0,)), ((), ())), preferred_element_type=F32)


def fill_ext(ext, lo, hidden, hi):
    ext[0:RIM, :] = lo[...]
    ext[RIM : RIM + ROWS, :] = hidden[...]
    ext[RIM + ROWS :, :] = hi[...]


def gather(source, ext, tile):
    return jnp.concatenate(
        [ext[pl.ds(pl.multiple_of(source[s, tile] * TB, TB), TB), :] for s in range(SLOTS)], axis=0
    )


def act(pre):
    sig = 0.5 * jnp.tanh(0.5 * pre) + 0.5
    return pre * sig, sig * (1.0 + pre * (1.0 - sig))


def scatter(source, adj_v, grad_agg, back, tile):
    part = dot(adj_v[tile], grad_agg)
    for s in range(SLOTS):
        at = pl.ds(pl.multiple_of(source[s, tile] * TB, TB), TB)
        back[at, :] += part[s * TB : (s + 1) * TB, :]


def edge_tiles(state, lo, hi, sems):
    copies = [
        pltpu.make_async_copy(state.at[pl.ds(0, RIM), :], lo, sems.at[0]),
        pltpu.make_async_copy(state.at[pl.ds(ROWS - RIM, RIM), :], hi, sems.at[1]),
    ]
    for copy in copies:
        copy.start()
    for copy in copies:
        copy.wait()


def prepare(count, blocks, state, w_self, w_nbr, adj, adj_v, own, hidden, *rest):
    kept, (raw, sems) = rest[: 2 * LAYERS], rest[2 * LAYERS :]
    loads = [(state, hidden), (w_self.at[0], kept[0]), (blocks, raw)]
    for layer in range(LAYERS):
        if layer:
            loads.append((w_self.at[layer], kept[layer]))
        loads.append((w_nbr.at[layer], kept[LAYERS + layer]))
    copies = [pltpu.make_async_copy(a, b, sems.at[i]) for i, (a, b) in enumerate(loads)]
    for copy in copies:
        copy.start()
    copies[0].wait()
    copies[1].wait()
    own[...] = dot(hidden[...], kept[0][...])
    copies[2].wait()
    for t in range(TILES):
        for s in range(SLOTS):
            live = (s < count[t]).astype(F32)
            block = (raw[t, s].astype(F32) * live).astype(BF)
            adj[t, :, s * TB : (s + 1) * TB] = block
            adj_v[t, s * TB : (s + 1) * TB, :] = block
    for copy in copies[3:]:
        copy.wait()


def forward_pair(source, adj, ext, own, hidden, w_nbr, pair):
    agg = jnp.concatenate([dot(adj[t], gather(source, ext, t)) for t in pair], axis=0).astype(BF)
    at = slice(pair[0] * TB, (pair[-1] + 1) * TB)
    pre = own[at, :] + dot(agg, w_nbr[...])
    gain, slope = act(pre)
    new = (hidden[at, :].astype(F32) + gain).astype(BF)
    return agg, new, slope


def forward_edge(source, adj, lo, hi, hidden, own, w_nbr, new_lo, new_hi, agg_e, slope_e, ext):
    fill_ext(ext, lo, hidden, hi)
    for i, (pair, out) in enumerate((((0, 1), new_lo), ((6, 7), new_hi))):
        agg, new, slope = forward_pair(source, adj, ext, own, hidden, w_nbr, pair)
        out[...] = new
        agg_e[i * RIM : (i + 1) * RIM, :] = agg
        slope_e[i * RIM : (i + 1) * RIM, :] = slope


def forward_mid(
    source, adj, lo, hi, hidden, own, w_nbr, new_lo, new_hi, agg_e, slope_e, w_self,
    new, agg_o, slope_o, own_o, ext,
):
    fill_ext(ext, lo, hidden, hi)
    for pair in ((2, 3), (4, 5)):
        at = slice(pair[0] * TB, (pair[-1] + 1) * TB)
        agg_o[at, :], new[at, :], slope_o[at, :] = forward_pair(
            source, adj, ext, own, hidden, w_nbr, pair
        )
    for i, edge in enumerate((new_lo, new_hi)):
        at = slice(i * (ROWS - RIM), i * (ROWS - RIM) + RIM)
        new[at, :] = edge[...]
        agg_o[at, :] = agg_e[i * RIM : (i + 1) * RIM, :]
        slope_o[at, :] = slope_e[i * RIM : (i + 1) * RIM, :]
    own_o[...] = dot(new[...], w_self[...])


def turn(
    source, adj, adj_v, lo, hi, hidden, own, w_nbr, cot,
    final, agg_o, gp_o, back, rim_lo, rim_hi, ext,
):
    fill_ext(ext, lo, hidden, hi)
    back[...] = jnp.zeros_like(back)
    for first in range(0, TILES, 2):
        pair = (first, first + 1)
        at = slice(pair[0] * TB, (pair[-1] + 1) * TB)
        agg, new, slope = forward_pair(source, adj, ext, own, hidden, w_nbr, pair)
        agg_o[at, :] = agg
        final[at, :] = new
        gp = (cot[at, :].astype(F32) * slope).astype(BF)
        gp_o[at, :] = gp
        grad_agg = dot_nt(gp, w_nbr[...]).astype(BF)
        for i, t in enumerate(pair):
            scatter(source, adj_v, grad_agg[i * TB : (i + 1) * TB], back, t)
    rim_lo[...] = back[0:RIM, :].astype(BF)
    rim_hi[...] = back[RIM + ROWS :, :].astype(BF)


def backward_mid(source, adj_v, gp, grad, back, w_self, slope, w_nbr, grad_o, gp_m, part):
    grad_o[...] = (
        grad[...].astype(F32) + dot_nt(gp[...], w_self[...]) + back[RIM : RIM + ROWS, :]
    )
    part[...] = jnp.zeros_like(part)
    for pair in ((2, 3), (4, 5)):
        at = slice(pair[0] * TB, (pair[-1] + 1) * TB)
        new = (grad_o[at, :] * slope[at, :]).astype(BF)
        gp_m[at.start - RIM : at.stop - RIM, :] = new
        grad_agg = dot_nt(new, w_nbr[...]).astype(BF)
        for i, t in enumerate(pair):
            scatter(source, adj_v, grad_agg[i * TB : (i + 1) * TB], part, t)


def backward_edge(
    source, adj_v, from_prev, from_next, grad, slope, w_nbr, gp_m, part,
    grad_o, gp_o, back, rim_lo, rim_hi,
):
    back[...] = part[...]
    for pair, come in (((0, 1), from_prev), ((6, 7), from_next)):
        at = slice(pair[0] * TB, (pair[-1] + 1) * TB)
        total = grad[at, :] + come[...].astype(F32)
        grad_o[at, :] = total
        new = (total * slope[at, :]).astype(BF)
        gp_o[at, :] = new
        grad_agg = dot_nt(new, w_nbr[...]).astype(BF)
        for i, t in enumerate(pair):
            scatter(source, adj_v, grad_agg[i * TB : (i + 1) * TB], back, t)
    rim_lo[...] = back[0:RIM, :].astype(BF)
    rim_hi[...] = back[RIM + ROWS :, :].astype(BF)
    grad_o[RIM : ROWS - RIM, :] = grad[RIM : ROWS - RIM, :]
    gp_o[RIM : ROWS - RIM, :] = gp_m[...]


def backward_first(gp, grad, back, w_self, grad_o):
    grad_o[...] = grad[...] + dot_nt(gp[...], w_self[...]) + back[RIM : RIM + ROWS, :]


def backward_last(grad, from_prev, from_next, out):
    out[0:RIM, :] = (grad[0:RIM, :] + from_prev[...].astype(F32)).astype(BF)
    out[RIM : ROWS - RIM, :] = grad[RIM : ROWS - RIM, :].astype(BF)
    out[ROWS - RIM :, :] = (grad[ROWS - RIM :, :] + from_next[...].astype(F32)).astype(BF)


def weight_grad(hidden, agg, gp, _, keep, send):
    core = lax.axis_index("core")
    for i, left in enumerate((hidden, agg)):
        full = dot_tn(left[...], gp[...]).astype(BF)
        low, high = full[:, : F // 2], full[:, F // 2 :]
        first = jnp.broadcast_to(core == 0, low.shape)
        keep[i * F : (i + 1) * F, :] = jnp.where(first, low, high)
        send[i * F : (i + 1) * F, :] = jnp.where(first, high, low)


def add_halves(mine, other, _, keep, send):
    y_bit = lax.rem(lax.div(lax.axis_index("dq"), jnp.int32(2)), jnp.int32(2))
    chip = (mine[...].astype(F32) + other[...].astype(F32)).astype(BF)
    low, high = chip[:, : F // 4], chip[:, F // 4 :]
    first = jnp.broadcast_to(y_bit == 0, low.shape)
    keep[...] = jnp.where(first, low, high)
    send[...] = jnp.where(first, high, low)


def all_parts(*refs):
    out = refs[-1]
    depth = out.shape[1] // 2
    sums = [(refs[2 * i][...].astype(F32) + refs[2 * i + 1][...].astype(F32)).astype(BF) for i in range(LAYERS)]
    for i in range(out.shape[0]):
        at = slice(i * depth, (i + 1) * depth)
        out[i, :depth, :] = sums[0][at, :]
        out[i, depth:, : F // 4] = sums[1][at, :]
        out[i, depth:, F // 4 :] = sums[2][at, :]


def sum_parts(parts, out):
    depth = parts.shape[1] // 2
    first = parts[0, :depth, :].astype(F32)
    halves = [None, None]
    for i in range(parts.shape[0]):
        if i:
            first += parts[i, :depth, :].astype(F32)
        half = parts[i, depth:, :].astype(F32)
        y_bit = i // 2 % 2
        halves[y_bit] = half if halves[y_bit] is None else halves[y_bit] + half
    low, high = halves
    total = jnp.concatenate(
        [
            first,
            jnp.concatenate([low[:, : F // 4], high[:, : F // 4]], axis=1),
            jnp.concatenate([low[:, F // 4 :], high[:, F // 4 :]], axis=1),
        ],
        axis=0,
    ).astype(BF)
    for i in range(out.shape[0]):
        out[i] = total


def unpack(factor, mine, other, *outs):
    core = lax.axis_index("core")
    depth = mine.shape[1] // LAYERS
    for layer in range(LAYERS):
        at = slice(layer * depth, (layer + 1) * depth)
        for i, out in enumerate(outs):
            group = slice(i * F // depth, (i + 1) * F // depth)
            a = mine[group, at, :].reshape(F, F // 2).astype(F32) * factor
            b = other[group, at, :].reshape(F, F // 2).astype(F32) * factor
            first = jnp.broadcast_to(core == 0, a.shape)
            out[layer, :, : F // 2] = jnp.where(first, a, b)
            out[layer, :, F // 2 :] = jnp.where(first, b, a)


def per_device(state, blocks, source, count, cotangent, w_self, w_nbr):
    state = state.reshape(ROWS, F)
    source = source.T
    cotangent = cotangent.reshape(ROWS, F)
    n_dom = lax.axis_size("dom")
    up = [(i, (i + 1) % n_dom) for i in range(n_dom)]
    down = [(i, (i - 1) % n_dom) for i in range(n_dom)]
    peers = lax.axis_size("dom") * lax.axis_size("dq")

    def swap(to_prev, to_next):
        return lax.ppermute(to_next, "dom", up), lax.ppermute(to_prev, "dom", down)

    wide = jax.ShapeDtypeStruct((RIM, F), BF)
    ext_scratch = pltpu.VMEM((EXT * TB, F), BF)

    lo, hi = swap(
        *call(edge_tiles, "edge_tiles", (wide, wide), [HB], [pltpu.SemaphoreType.DMA((2,))])(state)
    )
    adj, adj_v, own, hidden, *kept = call(
        prepare, "prepare",
        (
            pinned((TILES, TB, SLOTS * TB), BF), pinned((TILES, SLOTS * TB, TB), BF),
            pinned((ROWS, F), F32), pinned((ROWS, F), BF), *[pinned((F, F), BF)] * (2 * LAYERS),
        ),
        [SM] + [HB] * 4,
        [pltpu.VMEM((TILES, SLOTS, TB, TB), BF), pltpu.SemaphoreType.DMA((2 * LAYERS + 2,))],
    )(count, blocks, state, w_self, w_nbr)
    w_self, w_nbr = kept[:LAYERS], kept[LAYERS:]

    hiddens, aggs, slopes = [], [], []
    for layer in range(LAYERS - 1):
        new_lo, new_hi, agg_e, slope_e = call(
            forward_edge, f"forward_edge{layer}",
            (wide, wide, pinned((2 * RIM, F), BF), pinned((2 * RIM, F), F32)),
            [SM] + [VM] * 6, [ext_scratch],
        )(source, adj, lo, hi, hidden, own, w_nbr[layer])
        next_lo, next_hi = swap(new_lo, new_hi)
        new, agg, slope, own = call(
            forward_mid, f"forward_mid{layer}",
            (pinned((ROWS, F), BF), pinned((ROWS, F), BF), pinned((ROWS, F), F32), pinned((ROWS, F), F32)),
            [SM] + [VM] * 11, [ext_scratch],
        )(
            source, adj, lo, hi, hidden, own, w_nbr[layer], new_lo, new_hi, agg_e, slope_e,
            w_self[layer + 1],
        )
        hiddens.append(hidden)
        aggs.append(agg)
        slopes.append(slope)
        hidden, lo, hi = new, next_lo, next_hi

    hiddens.append(hidden)
    top = LAYERS - 1
    final, agg, gp, back, rim_lo, rim_hi = call(
        turn, "turn",
        (
            jax.ShapeDtypeStruct((ROWS, F), BF), pinned((ROWS, F), BF), pinned((ROWS, F), BF),
            pinned((EXT * TB, F), F32), wide, wide,
        ),
        [SM] + [VM] * 8, [ext_scratch],
    )(source, adj, adj_v, lo, hi, hidden, own, w_nbr[top], cotangent)
    aggs.append(agg)
    grad = cotangent

    half = jax.ShapeDtypeStruct((ROWS, F // 2), BF)
    quarter = jax.ShapeDtypeStruct((ROWS, F // 4), BF)
    sent = jax.ShapeDtypeStruct((peers, 2 * ROWS // peers, F // 2), BF)
    summed = jax.ShapeDtypeStruct((peers, LAYERS * ROWS // peers, F // 2), BF)
    flip = [(0, 1), (1, 0)]
    y_flip = [(i, i ^ 2) for i in range(lax.axis_size("dq"))]

    def weights(layer, gp, after):
        keep, send = call(weight_grad, f"weight_grad{layer}", (half, half), [VM] * 3 + [HB])(
            hiddens[layer], aggs[layer], gp, after
        )
        return keep, lax.ppermute(send, "core", flip)

    def spread(array):
        return lax.all_to_all(array, ("dom", "dq"), 0, 0, tiled=True)

    def pair(layer, keep, got, after):
        mine, yours = call(add_halves, f"add_halves{layer}", (quarter, quarter), [VM, VM, HB])(
            keep, got, after
        )
        return [mine, lax.ppermute(yours, "dq", y_flip)]

    halves, waiting = [], None
    for layer in range(top, -1, -1):
        from_prev, from_next = swap(rim_lo, rim_hi)
        if layer:
            grad, gp_m, part = call(
                backward_mid, f"backward_mid{layer}",
                (pinned((ROWS, F), F32), pinned((ROWS - 2 * RIM, F), BF), pinned((EXT * TB, F), F32)),
                [SM] + [VM] * 7,
            )(source, adj_v, gp, grad, back, w_self[layer], slopes[layer - 1], w_nbr[layer - 1])
            keep, got = weights(layer, gp, gp_m)
            if waiting:
                halves = pair(*waiting, gp_m)
            grad, gp, back, rim_lo, rim_hi = call(
                backward_edge, f"backward_edge{layer - 1}",
                (pinned((ROWS, F), F32), pinned((ROWS, F), BF), pinned((EXT * TB, F), F32), wide, wide),
                [SM] + [VM] * 8,
            )(source, adj_v, from_prev, from_next, grad, slopes[layer - 1], w_nbr[layer - 1], gp_m, part)
            waiting = layer, keep, got
    grad = call(
        backward_first, "backward_first", jax.ShapeDtypeStruct((ROWS, F), F32), [VM] * 4
    )(gp, grad, back, w_self[0])
    keep, got = weights(0, gp, grad)
    state_grad = call(
        backward_last, "backward_last", jax.ShapeDtypeStruct((ROWS, F), BF), [VM] * 3
    )(grad, from_prev, from_next)
    halves = pair(*waiting, rim_lo) + halves
    out = call(all_parts, "all_parts", sent, [VM] * 6)(keep, got, *halves)
    out, state_grad = lax.optimization_barrier((out, state_grad))
    out = call(sum_parts, "sum_parts", summed, [VM])(spread(out))
    whole = spread(out)
    other = lax.ppermute(whole, "core", flip)
    total_rows = lax.axis_size("dq") * lax.axis_size("core") * n_dom * ROWS
    grads = jax.ShapeDtypeStruct((LAYERS, F, F), F32)
    self_grad, nbr_grad = call(
        functools.partial(unpack, 1.0 / math.sqrt(total_rows)), "unpack", (grads, grads), [VM] * 2
    )(whole, other)
    return final[None], state_grad[None], self_grad, nbr_grad


def solution(mesh):
    dom, dp = mesh.devices.shape
    fine = Mesh(mesh.devices.reshape(dom, dp // 2, 2), ("dom", "dq", "core"))
    nodes = P(("dq", "core"), "dom", None)
    in_specs = (nodes, P("dom", None, None, None), P("dom", None), P("dom"), nodes, P(), P())
    out_specs = (nodes, nodes, P(), P())
    return jax.shard_map(
        per_device, mesh=fine, in_specs=in_specs, out_specs=out_specs, check_vma=False
    )
```

```python
import functools
import math

import jax
import jax.numpy as jnp
from jax import lax
from jax.experimental import pallas as pl
from jax.experimental.pallas import tpu as pltpu
from jax.sharding import Mesh
from jax.sharding import PartitionSpec as P

LAYERS = 3
TB = 128
TILES = 8
SLOTS = 4
HALO = 2
F = 512
ROWS = TILES * TB
RIM = HALO * TB
EXT = TILES + 2 * HALO
BF = jnp.bfloat16
F32 = jnp.float32
EDGE = (0, 1, 6, 7)
MID = (2, 3, 4, 5)
MB = 1 << 20

SM = pl.BlockSpec(memory_space=pltpu.SMEM)
VM = pl.BlockSpec(memory_space=pltpu.VMEM)
HB = pl.BlockSpec(memory_space=pltpu.HBM)


def pinned(shape, dtype):
    return pltpu.VMEM(shape, dtype)


def call(body, name, out_shape, in_specs, scratch=(), out_spec=VM, aliases={}, flops=1):
    return pl.pallas_call(
        body,
        name=name,
        out_shape=out_shape,
        in_specs=in_specs,
        out_specs=jax.tree.map(lambda _: out_spec, out_shape, is_leaf=lambda x: hasattr(x, "shape")),
        scratch_shapes=list(scratch),
        input_output_aliases=aliases,
        compiler_params=pltpu.CompilerParams(vmem_limit_bytes=12 * MB),
        cost_estimate=pl.CostEstimate(flops=flops, bytes_accessed=1, transcendentals=0),
    )


def rows(tile):
    return slice(tile * TB, (tile + 1) * TB)


def dot(a, b):
    return jnp.dot(a, b, preferred_element_type=F32)


def dot_nt(a, b):
    return lax.dot_general(a, b, (((1,), (1,)), ((), ())), preferred_element_type=F32)


def dot_tn(a, b):
    return lax.dot_general(a, b, (((0,), (0,)), ((), ())), preferred_element_type=F32)


def fill_ext(ext, lo, hidden, hi):
    ext[0:RIM, :] = lo[...]
    ext[RIM : RIM + ROWS, :] = hidden[...]
    ext[RIM + ROWS :, :] = hi[...]


def gather(source, ext, tile):
    return jnp.concatenate(
        [ext[pl.ds(pl.multiple_of(source[s, tile] * TB, TB), TB), :] for s in range(SLOTS)], axis=0
    )


def act(pre):
    sig = 0.5 * jnp.tanh(0.5 * pre) + 0.5
    return pre * sig, sig * (1.0 + pre * (1.0 - sig))


def scatter(source, adj_v, grad_agg, back, tile):
    part = dot(adj_v[tile], grad_agg)
    for s in range(SLOTS):
        at = pl.ds(pl.multiple_of(source[s, tile] * TB, TB), TB)
        back[at, :] += part[s * TB : (s + 1) * TB, :]


def edge_tiles(state, lo, hi, sems):
    copies = [
        pltpu.make_async_copy(state.at[pl.ds(0, RIM), :], lo, sems.at[0]),
        pltpu.make_async_copy(state.at[pl.ds(ROWS - RIM, RIM), :], hi, sems.at[1]),
    ]
    for copy in copies:
        copy.start()
    for copy in copies:
        copy.wait()


def prepare(count, blocks, state, w_self, w_nbr, adj, adj_v, own, hidden, *rest):
    kept, (raw, sems) = rest[: 2 * LAYERS], rest[2 * LAYERS :]
    loads = [(state, hidden), (w_self.at[0], kept[0]), (blocks, raw)]
    for layer in range(LAYERS):
        if layer:
            loads.append((w_self.at[layer], kept[layer]))
        loads.append((w_nbr.at[layer], kept[LAYERS + layer]))
    copies = [pltpu.make_async_copy(a, b, sems.at[i]) for i, (a, b) in enumerate(loads)]
    for copy in copies:
        copy.start()
    copies[0].wait()
    copies[1].wait()
    own[...] = dot(hidden[...], kept[0][...])
    copies[2].wait()
    for t in range(TILES):
        for s in range(SLOTS):
            live = (s < count[t]).astype(F32)
            block = (raw[t, s].astype(F32) * live).astype(BF)
            adj[t, :, s * TB : (s + 1) * TB] = block
            adj_v[t, s * TB : (s + 1) * TB, :] = block
    for copy in copies[3:]:
        copy.wait()


def forward_pair(source, adj, ext, own, hidden, w_nbr, pair):
    agg = jnp.concatenate([dot(adj[t], gather(source, ext, t)) for t in pair], axis=0).astype(BF)
    at = slice(pair[0] * TB, (pair[-1] + 1) * TB)
    pre = own[at, :] + dot(agg, w_nbr[...])
    gain, slope = act(pre)
    new = (hidden[at, :].astype(F32) + gain).astype(BF)
    return agg, new, slope


def forward_edge(source, adj, lo, hi, hidden, own, w_nbr, new_lo, new_hi, agg_e, slope_e, ext):
    fill_ext(ext, lo, hidden, hi)
    for i, (pair, out) in enumerate((((0, 1), new_lo), ((6, 7), new_hi))):
        agg, new, slope = forward_pair(source, adj, ext, own, hidden, w_nbr, pair)
        out[...] = new
        agg_e[i * RIM : (i + 1) * RIM, :] = agg
        slope_e[i * RIM : (i + 1) * RIM, :] = slope


def forward_mid(
    source, adj, lo, hi, hidden, own, w_nbr, new_lo, new_hi, agg_e, slope_e, w_self,
    new, agg_o, slope_o, own_o, ext,
):
    fill_ext(ext, lo, hidden, hi)
    for pair in ((2, 3), (4, 5)):
        at = slice(pair[0] * TB, (pair[-1] + 1) * TB)
        agg_o[at, :], new[at, :], slope_o[at, :] = forward_pair(
            source, adj, ext, own, hidden, w_nbr, pair
        )
    for i, edge in enumerate((new_lo, new_hi)):
        at = slice(i * (ROWS - RIM), i * (ROWS - RIM) + RIM)
        new[at, :] = edge[...]
        agg_o[at, :] = agg_e[i * RIM : (i + 1) * RIM, :]
        slope_o[at, :] = slope_e[i * RIM : (i + 1) * RIM, :]
    own_o[...] = dot(new[...], w_self[...])


def turn(
    source, adj, adj_v, lo, hi, hidden, own, w_nbr, cot,
    final, agg_o, gp_o, back, rim_lo, rim_hi, ext,
):
    fill_ext(ext, lo, hidden, hi)
    back[...] = jnp.zeros_like(back)
    for first in range(0, TILES, 2):
        pair = (first, first + 1)
        at = slice(pair[0] * TB, (pair[-1] + 1) * TB)
        agg, new, slope = forward_pair(source, adj, ext, own, hidden, w_nbr, pair)
        agg_o[at, :] = agg
        final[at, :] = new
        gp = (cot[at, :].astype(F32) * slope).astype(BF)
        gp_o[at, :] = gp
        grad_agg = dot_nt(gp, w_nbr[...]).astype(BF)
        for i, t in enumerate(pair):
            scatter(source, adj_v, grad_agg[i * TB : (i + 1) * TB], back, t)
    rim_lo[...] = back[0:RIM, :].astype(BF)
    rim_hi[...] = back[RIM + ROWS :, :].astype(BF)


def backward_mid(source, adj_v, gp, grad, back, w_self, slope, w_nbr, grad_o, gp_m, part):
    grad_o[...] = (
        grad[...].astype(F32) + dot_nt(gp[...], w_self[...]) + back[RIM : RIM + ROWS, :]
    )
    part[...] = jnp.zeros_like(part)
    for pair in ((2, 3), (4, 5)):
        at = slice(pair[0] * TB, (pair[-1] + 1) * TB)
        new = (grad_o[at, :] * slope[at, :]).astype(BF)
        gp_m[at.start - RIM : at.stop - RIM, :] = new
        grad_agg = dot_nt(new, w_nbr[...]).astype(BF)
        for i, t in enumerate(pair):
            scatter(source, adj_v, grad_agg[i * TB : (i + 1) * TB], part, t)


def backward_edge(
    source, adj_v, from_prev, from_next, grad, slope, w_nbr, gp_m, part,
    grad_o, gp_o, back, rim_lo, rim_hi,
):
    back[...] = part[...]
    for pair, come in (((0, 1), from_prev), ((6, 7), from_next)):
        at = slice(pair[0] * TB, (pair[-1] + 1) * TB)
        total = grad[at, :] + come[...].astype(F32)
        grad_o[at, :] = total
        new = (total * slope[at, :]).astype(BF)
        gp_o[at, :] = new
        grad_agg = dot_nt(new, w_nbr[...]).astype(BF)
        for i, t in enumerate(pair):
            scatter(source, adj_v, grad_agg[i * TB : (i + 1) * TB], back, t)
    rim_lo[...] = back[0:RIM, :].astype(BF)
    rim_hi[...] = back[RIM + ROWS :, :].astype(BF)
    grad_o[RIM : ROWS - RIM, :] = grad[RIM : ROWS - RIM, :]
    gp_o[RIM : ROWS - RIM, :] = gp_m[...]


def backward_first(gp, grad, back, w_self, grad_o):
    grad_o[...] = grad[...] + dot_nt(gp[...], w_self[...]) + back[RIM : RIM + ROWS, :]


def backward_last(grad, from_prev, from_next, out, ready, sem):
    ready[0:RIM, :] = (grad[0:RIM, :] + from_prev[...].astype(F32)).astype(BF)
    ready[RIM : ROWS - RIM, :] = grad[RIM : ROWS - RIM, :].astype(BF)
    ready[ROWS - RIM :, :] = (grad[ROWS - RIM :, :] + from_next[...].astype(F32)).astype(BF)
    copy = pltpu.make_async_copy(ready, out, sem)
    copy.start()
    copy.wait()


def weight_grad(hidden, agg, gp, _, keep, send):
    core = lax.axis_index("core")
    for i, left in enumerate((hidden, agg)):
        full = dot_tn(left[...], gp[...]).astype(BF)
        low, high = full[:, : F // 2], full[:, F // 2 :]
        first = jnp.broadcast_to(core == 0, low.shape)
        keep[i * F : (i + 1) * F, :] = jnp.where(first, low, high)
        send[i * F : (i + 1) * F, :] = jnp.where(first, high, low)


def add_halves(mine, other, _, keep, send):
    y_bit = lax.rem(lax.div(lax.axis_index("dq"), jnp.int32(2)), jnp.int32(2))
    chip = (mine[...].astype(F32) + other[...].astype(F32)).astype(BF)
    low, high = chip[:, : F // 4], chip[:, F // 4 :]
    first = jnp.broadcast_to(y_bit == 0, low.shape)
    keep[...] = jnp.where(first, low, high)
    send[...] = jnp.where(first, high, low)


def upper_parts(mine_1, other_1, mine_2, other_2, out):
    for i, (a, b) in enumerate(((mine_1, other_1), (mine_2, other_2))):
        out[:, i * F // 4 : (i + 1) * F // 4] = (a[...].astype(F32) + b[...].astype(F32)).astype(BF)


def all_parts(mine, other, upper, _, out):
    depth = out.shape[1] // 2
    base = (mine[...].astype(F32) + other[...].astype(F32)).astype(BF)
    for i in range(out.shape[0]):
        at = slice(i * depth, (i + 1) * depth)
        out[i, :depth, :] = base[at, :]
        out[i, depth:, :] = upper[at, :]


def sum_parts(parts, out):
    depth = parts.shape[1] // 2
    first = parts[0, :depth, :].astype(F32)
    halves = [None, None]
    for i in range(parts.shape[0]):
        if i:
            first += parts[i, :depth, :].astype(F32)
        half = parts[i, depth:, :].astype(F32)
        y_bit = i // 2 % 2
        halves[y_bit] = half if halves[y_bit] is None else halves[y_bit] + half
    low, high = halves
    total = jnp.concatenate(
        [
            first,
            jnp.concatenate([low[:, : F // 4], high[:, : F // 4]], axis=1),
            jnp.concatenate([low[:, F // 4 :], high[:, F // 4 :]], axis=1),
        ],
        axis=0,
    ).astype(BF)
    for i in range(out.shape[0]):
        out[i] = total


def unpack(factor, flip, half, *refs):
    self_o, nbr_o, ready, sems = refs[-4:]
    core = lax.axis_index("core")
    start = pl.multiple_of((1 - core if flip else core) * (F // 2), F // 2)
    depth = half.shape[1] // LAYERS
    copies = []
    for layer in range(LAYERS):
        at = slice(layer * depth, (layer + 1) * depth)
        for i, out in enumerate((self_o, nbr_o)):
            group = slice(i * F // depth, (i + 1) * F // depth)
            ready[layer, i] = half[group, at, :].reshape(F, F // 2).astype(F32) * factor
            copies.append(
                pltpu.make_async_copy(
                    ready.at[layer, i], out.at[layer, :, pl.ds(start, F // 2)], sems.at[layer, i]
                )
            )
            copies[-1].start()
    for copy in copies:
        copy.wait()


def per_device(state, blocks, source, count, cotangent, w_self, w_nbr):
    state = state.reshape(ROWS, F)
    source = source.T
    cotangent = cotangent.reshape(ROWS, F)
    n_dom = lax.axis_size("dom")
    up = [(i, (i + 1) % n_dom) for i in range(n_dom)]
    down = [(i, (i - 1) % n_dom) for i in range(n_dom)]
    peers = lax.axis_size("dom") * lax.axis_size("dq")

    def swap(to_prev, to_next):
        return lax.ppermute(to_next, "dom", up), lax.ppermute(to_prev, "dom", down)

    wide = jax.ShapeDtypeStruct((RIM, F), BF)
    ext_scratch = pltpu.VMEM((EXT * TB, F), BF)

    lo, hi = swap(
        *call(edge_tiles, "edge_tiles", (wide, wide), [HB], [pltpu.SemaphoreType.DMA((2,))])(state)
    )
    adj, adj_v, own, hidden, *kept = call(
        prepare, "prepare",
        (
            pinned((TILES, TB, SLOTS * TB), BF), pinned((TILES, SLOTS * TB, TB), BF),
            pinned((ROWS, F), F32), pinned((ROWS, F), BF), *[pinned((F, F), BF)] * (2 * LAYERS),
        ),
        [SM] + [HB] * 4,
        [pltpu.VMEM((TILES, SLOTS, TB, TB), BF), pltpu.SemaphoreType.DMA((2 * LAYERS + 2,))],
    )(count, blocks, state, w_self, w_nbr)
    w_self, w_nbr = kept[:LAYERS], kept[LAYERS:]

    hiddens, aggs, slopes = [], [], []
    for layer in range(LAYERS - 1):
        new_lo, new_hi, agg_e, slope_e = call(
            forward_edge, f"forward_edge{layer}",
            (wide, wide, pinned((2 * RIM, F), BF), pinned((2 * RIM, F), F32)),
            [SM] + [VM] * 6, [ext_scratch],
        )(source, adj, lo, hi, hidden, own, w_nbr[layer])
        next_lo, next_hi = swap(new_lo, new_hi)
        new, agg, slope, own = call(
            forward_mid, f"forward_mid{layer}",
            (pinned((ROWS, F), BF), pinned((ROWS, F), BF), pinned((ROWS, F), F32), pinned((ROWS, F), F32)),
            [SM] + [VM] * 11, [ext_scratch],
        )(
            source, adj, lo, hi, hidden, own, w_nbr[layer], new_lo, new_hi, agg_e, slope_e,
            w_self[layer + 1],
        )
        hiddens.append(hidden)
        aggs.append(agg)
        slopes.append(slope)
        hidden, lo, hi = new, next_lo, next_hi

    hiddens.append(hidden)
    top = LAYERS - 1
    final, agg, gp, back, rim_lo, rim_hi = call(
        turn, "turn",
        (
            jax.ShapeDtypeStruct((ROWS, F), BF), pinned((ROWS, F), BF), pinned((ROWS, F), BF),
            pinned((EXT * TB, F), F32), wide, wide,
        ),
        [SM] + [VM] * 8, [ext_scratch],
    )(source, adj, adj_v, lo, hi, hidden, own, w_nbr[top], cotangent)
    aggs.append(agg)
    grad = cotangent

    half = jax.ShapeDtypeStruct((ROWS, F // 2), BF)
    quarter = jax.ShapeDtypeStruct((ROWS, F // 4), BF)
    sent = jax.ShapeDtypeStruct((peers, 2 * ROWS // peers, F // 2), BF)
    summed = jax.ShapeDtypeStruct((peers, LAYERS * ROWS // peers, F // 2), BF)
    flip = [(0, 1), (1, 0)]
    y_flip = [(i, i ^ 2) for i in range(lax.axis_size("dq"))]

    def weights(layer, gp, after):
        keep, send = call(weight_grad, f"weight_grad{layer}", (half, half), [VM] * 3 + [HB])(
            hiddens[layer], aggs[layer], gp, after
        )
        return keep, lax.ppermute(send, "core", flip)

    def spread(array):
        return lax.all_to_all(array, ("dom", "dq"), 0, 0, tiled=True)

    def pair(layer, keep, got, after):
        mine, yours = call(add_halves, f"add_halves{layer}", (quarter, quarter), [VM, VM, HB])(
            keep, got, after
        )
        return [mine, lax.ppermute(yours, "dq", y_flip)]

    halves, waiting = [], None
    for layer in range(top, -1, -1):
        from_prev, from_next = swap(rim_lo, rim_hi)
        if layer:
            grad, gp_m, part = call(
                backward_mid, f"backward_mid{layer}",
                (pinned((ROWS, F), F32), pinned((ROWS - 2 * RIM, F), BF), pinned((EXT * TB, F), F32)),
                [SM] + [VM] * 7,
            )(source, adj_v, gp, grad, back, w_self[layer], slopes[layer - 1], w_nbr[layer - 1])
            keep, got = weights(layer, gp, gp_m)
            if waiting:
                halves = pair(*waiting, gp_m)
            grad, gp, back, rim_lo, rim_hi = call(
                backward_edge, f"backward_edge{layer - 1}",
                (pinned((ROWS, F), F32), pinned((ROWS, F), BF), pinned((EXT * TB, F), F32), wide, wide),
                [SM] + [VM] * 8, flops=9 * 10**9,
            )(source, adj_v, from_prev, from_next, grad, slopes[layer - 1], w_nbr[layer - 1], gp_m, part)
            waiting = layer, keep, got
    grad = call(
        backward_first, "backward_first", jax.ShapeDtypeStruct((ROWS, F), F32), [VM] * 4
    )(gp, grad, back, w_self[0])
    halves = pair(*waiting, rim_lo) + halves
    keep, got = weights(0, gp, halves[0])
    state_grad = call(
        backward_last, "backward_last", jax.ShapeDtypeStruct((ROWS, F), BF), [VM] * 3,
        [pltpu.VMEM((ROWS, F), BF), pltpu.SemaphoreType.DMA], HB, flops=9 * 10**9,
    )(grad, from_prev, from_next)
    upper = call(upper_parts, "upper_parts", half, [VM] * 4, flops=9 * 10**9)(*halves)
    out = call(all_parts, "all_parts", sent, [VM] * 3 + [HB])(keep, got, upper, state_grad)
    out = call(sum_parts, "sum_parts", summed, [VM])(spread(out))
    whole = spread(out)
    other = lax.ppermute(whole, "core", flip)
    total_rows = lax.axis_size("dq") * lax.axis_size("core") * n_dom * ROWS
    grads = jax.ShapeDtypeStruct((LAYERS, F, F), F32)
    factor = 1.0 / math.sqrt(total_rows)
    scratch = [pltpu.VMEM((LAYERS, 2, F, F // 2), F32), pltpu.SemaphoreType.DMA((LAYERS, 2))]
    own = call(
        functools.partial(unpack, factor, False), "unpack_own", (grads, grads), [VM], scratch, HB
    )(whole)
    self_grad, nbr_grad = call(
        functools.partial(unpack, factor, True), "unpack_other", (grads, grads), [VM, HB, HB],
        scratch, HB, {1: 0, 2: 1},
    )(other, *own)
    return final[None], state_grad[None], self_grad, nbr_grad


def solution(mesh):
    dom, dp = mesh.devices.shape
    fine = Mesh(mesh.devices.reshape(dom, dp // 2, 2), ("dom", "dq", "core"))
    nodes = P(("dq", "core"), "dom", None)
    in_specs = (nodes, P("dom", None, None, None), P("dom", None), P("dom"), nodes, P(), P())
    out_specs = (nodes, nodes, P(), P())
    return jax.shard_map(
        per_device, mesh=fine, in_specs=in_specs, out_specs=out_specs, check_vma=False
    )
```
